32 devices in a mesh: ctx: 8 (over z, x), head: 4 (over y, core).
Axes of the slice: x: 2, y: 2, z: 4, core: 2. Of those that a mesh axis runs over, the one named last changes fastest.
Arguments:
- tokens: bfloat16 [2048, 256], P('ctx'), may hold values from -6 to 6
- in_gain: float32 [256], replicated, may hold values from 0.1 to 1.9
- w_uvqk: bfloat16 [256, 8, 128], P(None, 'head'), may hold values from -0.375 to 0.375
- w_out: bfloat16 [256, 256], P('head'), may hold values from -0.375 to 0.375
- grad_out: bfloat16 [2048, 256], P('ctx'), may hold values from -6 to 6
- lengths: int32 [3], replicated, may hold values from 1 to 1024, 2048 in all
- block_order: int32 [16], replicated, may hold values from 0 to 15, each once
Outputs:
- tokens_grad: bfloat16 [2048, 256], P('ctx')
- uvqk_grad: float32 [256, 8, 128], P('ctx', 'head')
- out_weight_grad: float32 [256, 256], P('head', 'ctx')
The draws below stay inside these ranges and needn't reach their ends.
Inputs may be any that keep to these rules, and one draw needn't show every extreme that they name: User history lengths in loader order, summing to 2048; the longest is exactly 1024. `block_order`: a permutation of the 16 blocks.
All inputs are finite; a program needn't handle non-finite values.
Results may differ from the reference program's by a relative error of at most 0.0075.
Values may be sent and summed in bfloat16 or wider, within the bound.
A program may use at most 64 MiB of HBM per device.

```python
import math
import jax
import jax.numpy as jnp
import numpy as np
from jax import lax

D = 256
H = 8
DH = 32
BLOCK = 128
USERS = 3
TOKENS = 2048
LMAX = 1024
NBLK = 16


def block_levels(rng, dims, split, least, top_value):
    def one(dim, parts):
        steps = jax.random.uniform(jax.random.fold_in(jax.random.fold_in(rng, 6), dim), (parts,), jnp.float32, least / len(split), top_value / len(split))
        return jnp.repeat(jnp.exp(steps), dims[dim] // parts).reshape((-1,) + (1,) * (len(dims) - dim - 1))

    loudness = one(*split[0])
    for cut in split[1:]:
        loudness = loudness * one(*cut)
    return loudness


def length_profile(amount, total, limit, slope):
    portions = [(1 << 20) // math.isqrt(rank ** slope) + 1 for rank in range(2, amount + 1)]
    rest, given = total - limit - (amount - 1), [1] * (amount - 1)
    while rest > 0:
        movable = [i for i in range(amount - 1) if given[i] < limit]
        pool, budget = sum([portions[i] for i in movable]), rest
        for i in movable:
            more = min(limit - given[i], max(1, budget * portions[i] // pool), rest)
            given[i] = given[i] + more
            rest = rest - more
    return np.array([limit] + given)


def uneven(stream_key, amount, total, bound, slope):
    if amount == 2:
        one = jax.random.randint(stream_key, (), max(1, total - bound), min(bound, total - 1) + 1)
        return jnp.stack([one, total - one])
    sizes = jnp.asarray(length_profile(amount, total, bound, slope), jnp.int32)
    twos = (amount - 1) // 2
    source_of, taker = sizes[1:1 + 2 * twos:2], sizes[2:2 + 2 * twos:2]
    slack = jnp.minimum(source_of - 1, bound - taker)
    shifted = jax.random.randint(jax.random.fold_in(stream_key, 1), (twos,), 0, 1 << 20) % (slack + 1)
    sizes = sizes.at[1:1 + 2 * twos:2].set(source_of - shifted).at[2:2 + 2 * twos:2].set(taker + shifted)
    return sizes[jax.random.permutation(jax.random.fold_in(stream_key, 2), amount)]


def noise(key, dims, deviation, bound, pieces=(), kind=jnp.bfloat16):
    result = jax.random.normal(key, dims, jnp.float32) * deviation
    if len(pieces) > 0:
        result = block_levels(key, dims, pieces, -0.22, 0.18) * result
    return jnp.clip(result, min=-bound, max=bound).astype(kind)


def setup_inputs(seed: int = 0) -> dict:
    keys = jax.random.split(jax.random.key(seed), 8)
    tokens = noise(keys[0], (TOKENS, D), 1.0, 6.0, ((0, 8),))
    in_gain = jnp.clip(1.0 + 0.18 * jax.random.normal(keys[1], (D,), jnp.float32), 0.1, 1.9)
    w_uvqk = noise(keys[2], (D, H, 4 * DH), D ** -0.5, 0.375, ((1, 4),))
    w_out = noise(keys[3], (H * DH, D), (H * DH) ** -0.5, 0.375, ((0, 4),))
    grad_out = noise(keys[4], (TOKENS, D), 1.0, 6.0, ((0, 8),))
    lengths = uneven(keys[5], USERS, TOKENS, LMAX, 0).astype(jnp.int32)
    block_order = jax.random.permutation(keys[6], NBLK).astype(jnp.int32)
    return {"tokens": tokens, "in_gain": in_gain, "w_uvqk": w_uvqk, "w_out": w_out, "grad_out": grad_out, "lengths": lengths, "block_order": block_order}


def rounded(values):
    return lax.optimization_barrier(values.astype(jnp.bfloat16)).astype(jnp.float32)

def silu_slope(values):
    sigmoid = jax.nn.sigmoid(values)
    return sigmoid * (1.0 + values * (1.0 - sigmoid))

def reference(tokens, in_gain, w_uvqk, w_out, grad_out, lengths, block_order):
    all_rows = jnp.arange(TOKENS, dtype=jnp.int32)
    events = block_order[all_rows // BLOCK] * BLOCK + all_rows % BLOCK
    ends = jnp.cumsum(lengths).astype(jnp.int32)
    owners = lax.optimization_barrier(jnp.sum((events[:, None] >= ends[None, :]).astype(jnp.int32), axis=1))
    float_in = tokens.astype(jnp.float32)
    row_mean = lax.optimization_barrier(jnp.mean(float_in, axis=1, keepdims=True))
    centered = float_in - row_mean
    inv_std = lax.rsqrt(lax.optimization_barrier(jnp.mean(centered * centered, axis=1, keepdims=True)) + 1e-05)
    normed = centered * inv_std
    scaled_in = (normed * in_gain).astype(jnp.bfloat16)
    pre_act = jnp.einsum('td,dhc->thc', scaled_in.astype(jnp.float32), w_uvqk.astype(jnp.float32))
    activ = jax.nn.silu(pre_act).astype(jnp.bfloat16).astype(jnp.float32)
    units_f = activ[..., :DH]
    values_f = activ[..., DH:2 * DH]
    queries_f = activ[..., 2 * DH:3 * DH]
    keys_f = activ[..., 3 * DH:]
    attn_width = H * DH
    score_scale = 1.0 / LMAX
    q_block = math.gcd(TOKENS, 128)
    block_count = TOKENS // q_block

    def block_mask(index):
        first = index * q_block
        ev_block = lax.dynamic_slice_in_dim(events, first, q_block)
        ow_block = lax.dynamic_slice_in_dim(owners, first, q_block)
        return ((ow_block[:, None] == owners[None, :]) & (events[None, :] <= ev_block[:, None])).astype(jnp.float32)

    def forward_block(index):
        query_part = lax.dynamic_slice_in_dim(queries_f, index * q_block, q_block, 0)
        scores = jnp.einsum('qhd,khd->hqk', query_part, keys_f)
        weights = rounded(jax.nn.silu(scores) * score_scale * block_mask(index))
        return jnp.einsum('hqk,khd->qhd', weights, values_f)
    indices = jnp.arange(block_count, dtype=jnp.int32)
    attended = lax.map(forward_block, indices).reshape(TOKENS, attn_width)
    attn_mean = lax.optimization_barrier(jnp.mean(attended, axis=1, keepdims=True))
    attn_var = lax.optimization_barrier(jnp.mean(attended * attended, axis=1, keepdims=True)) - attn_mean * attn_mean
    attn_inv = lax.rsqrt(attn_var + 1e-05)
    attn_norm = (attended - attn_mean) * attn_inv
    units_flat = units_f.reshape(TOKENS, attn_width)
    gated = (attn_norm * units_flat).astype(jnp.bfloat16)
    gated_grad = jnp.dot(grad_out, w_out.T, preferred_element_type=jnp.float32)
    out_weight_grad = jnp.dot(gated.T, grad_out, preferred_element_type=jnp.float32)
    units_grad = gated_grad * attn_norm
    norm_grad = gated_grad * units_flat
    attn_grad = (norm_grad - lax.optimization_barrier(jnp.mean(norm_grad, axis=1, keepdims=True)) - attn_norm * lax.optimization_barrier(jnp.mean(norm_grad * attn_norm, axis=1, keepdims=True))) * attn_inv
    attn_grad_f = attn_grad.astype(jnp.bfloat16).astype(jnp.float32).reshape(TOKENS, H, DH)

    def backward_block(totals, index):
        key_grad, value_grad = totals
        first = index * q_block
        query_part = lax.dynamic_slice_in_dim(queries_f, first, q_block, 0)
        grad_part = lax.dynamic_slice_in_dim(attn_grad_f, first, q_block, 0)
        live = block_mask(index)
        scores = jnp.einsum('qhd,khd->hqk', query_part, keys_f)
        sigmoid = jax.nn.sigmoid(scores)
        weights = rounded(jax.nn.silu(scores) * score_scale * live)
        weight_grad = jnp.einsum('qhd,khd->hqk', grad_part, values_f)
        score_grad = rounded(weight_grad * sigmoid * (1.0 + scores * (1.0 - sigmoid)) * score_scale * live)
        query_grad = jnp.einsum('hqk,khd->qhd', score_grad, keys_f)
        key_grad = key_grad + jnp.einsum('hqk,qhd->khd', score_grad, query_part)
        value_grad = value_grad + jnp.einsum('hqk,qhd->khd', weights, grad_part)
        return ((key_grad, value_grad), query_grad)
    zero_heads = jnp.zeros((TOKENS, H, DH), jnp.float32)
    (key_grad, value_grad), query_grads = lax.scan(backward_block, (zero_heads, zero_heads), indices)
    query_grad = query_grads.reshape(TOKENS, H, DH)
    act_grad = jnp.concatenate([units_grad.reshape(TOKENS, H, DH), value_grad, query_grad, key_grad], axis=2)
    pre_grad = (act_grad * silu_slope(pre_act)).astype(jnp.bfloat16).astype(jnp.float32)
    input_grad = jnp.einsum('thc,dhc->td', pre_grad, w_uvqk.astype(jnp.float32))
    uvqk_grad = jnp.einsum('td,thc->dhc', scaled_in.astype(jnp.float32), pre_grad)
    scaled_grad = input_grad * in_gain
    tokens_grad = grad_out.astype(jnp.float32) + (scaled_grad - lax.optimization_barrier(jnp.mean(scaled_grad, axis=1, keepdims=True)) - normed * lax.optimization_barrier(jnp.mean(scaled_grad * normed, axis=1, keepdims=True))) * inv_std
    return (tokens_grad.astype(jnp.bfloat16), uvqk_grad, out_weight_grad)
```

```python
import functools

import jax
import jax.numpy as jnp
from jax import lax
from jax.experimental import pallas as pl
from jax.experimental.pallas import tpu as pltpu
from jax.sharding import PartitionSpec as P

F32 = jnp.float32
BF16 = jnp.bfloat16
LANES = 128
MESH = pl.DeviceIdType.MESH


def dot_nt(a, b):
    return lax.dot_general(a, b, (((1,), (1,)), ((), ())), preferred_element_type=F32)


def dot_nn(a, b):
    return lax.dot_general(a, b, (((1,), (0,)), ((), ())), preferred_element_type=F32)


def dot_tn(a, b):
    return lax.dot_general(a, b, (((0,), (0,)), ((), ())), preferred_element_type=F32)


def silu_parts(scores, scale):
    sigma = 0.5 * jnp.tanh(0.5 * scores) + 0.5
    silu = scores * sigma
    return (silu * scale).astype(BF16), (sigma + silu * (1.0 - sigma)) * scale


def kernel(
    n, m, block, users, score_scale, keep,
    lengths_ref, order_ref, tokens_ref, gain_ref, w_ref, wout_ref, gout_ref,
    tok_ref, uvqk_ref, wo_ref,
    kv_all, q_all, ag_all, st_all, wo_send, wo_recv, uv_send, uv_recv,
    ip_send, ip_recv, tg_all, normed_ref, istd_ref, pre_ref, evq_ref, stq_ref,
    acc_ref, acck_ref, accv_ref, dq_ref, wk_ref, dk_ref,
    c_send, c_recv, h_send, h_recv,
):
    me = lax.axis_index("ctx")
    hd = lax.axis_index("head")
    rows, width = tokens_ref.shape
    half = rows // 2
    part = rows // m
    chunk = width // n

    barrier = pltpu.get_barrier_semaphore()

    def greet_ctx(s, c):
        pl.semaphore_signal(
            barrier, inc=1, device_id={"ctx": lax.rem(me + s, n)}, device_id_type=MESH
        )
        return c

    def greet_head(s, c):
        pl.semaphore_signal(
            barrier, inc=1, device_id={"head": lax.rem(hd + s, m)}, device_id_type=MESH
        )
        return c

    lax.fori_loop(1, n, greet_ctx, 0)
    lax.fori_loop(1, m, greet_head, 0)

    def ctx_copy(kind, src, dst, slot, sem, peer):
        return pltpu.make_async_remote_copy(
            src_ref=src.at[slot],
            dst_ref=dst.at[sem],
            send_sem=c_send.at[kind, slot if src is not dst else peer],
            recv_sem=c_recv.at[kind, sem],
            device_id={"ctx": peer},
            device_id_type=MESH,
        )

    def head_copy(kind, src, dst, slot, sem, peer):
        return pltpu.make_async_remote_copy(
            src_ref=src.at[slot],
            dst_ref=dst.at[sem],
            send_sem=h_send.at[kind, slot if src is not dst else peer],
            recv_sem=h_recv.at[kind, sem],
            device_id={"head": peer},
            device_id_type=MESH,
        )

    def spread(copy, kind, src, dst, mine, count, scatter):
        def step(s, c):
            peer = lax.rem(mine + s, count)
            copy(kind, src, dst, peer if scatter else mine, mine, peer).start()
            return c

        lax.fori_loop(1, count, step, 0)

    def arrived(copy, kind, src, dst, mine, count, scatter, s):
        origin = lax.rem(mine + count - s, count)
        copy(kind, src, dst, origin if scatter else mine, origin, origin).wait_recv()
        return origin

    def sent(copy, kind, src, dst, mine, count, scatter):
        def step(s, c):
            peer = lax.rem(mine + s, count)
            copy(kind, src, dst, peer if scatter else mine, mine, peer).wait_send()
            return c

        lax.fori_loop(1, count, step, 0)

    x = tokens_ref[...].astype(F32)
    centered = x - jnp.mean(x, axis=1, keepdims=True)
    istd = lax.rsqrt(jnp.mean(centered * centered, axis=1, keepdims=True) + 1e-05)
    normed = centered * istd
    normed_ref[...] = normed
    istd_ref[...] = jnp.broadcast_to(istd, (rows, LANES))
    scaled_in = (normed * gain_ref[...]).astype(BF16)
    pre = dot_nn(scaled_in, w_ref[...])
    pre_ref[...] = pre
    act = pre * (0.5 * jnp.tanh(0.5 * pre) + 0.5)
    act_a = act[:, :LANES].astype(BF16)
    act_b = act[:, LANES:].astype(BF16)
    kv_all[me] = act_b
    lane = lax.broadcasted_iota(jnp.int32, (rows, LANES), 1)
    low = lane < 64
    head0 = (lane & 32) == 0
    low_half = lax.broadcasted_iota(jnp.int32, (half, LANES), 1) < 64
    q_all[me] = jnp.where(
        low_half, pltpu.roll(act[:half, :LANES], 64, 1), act[half:, :LANES]
    ).astype(BF16)

    pl.semaphore_wait(barrier, n + m - 2)
    spread(ctx_copy, 0, kv_all, kv_all, me, n, False)
    spread(ctx_copy, 1, q_all, q_all, me, n, False)

    ends = []
    running = jnp.int32(0)
    for u in range(users):
        running = running + lengths_ref[u]
        ends.append(running)

    def starts(events):
        begin = jnp.zeros_like(events)
        for end in ends:
            begin = jnp.where(events >= end, end, begin)
        return begin

    row = lax.broadcasted_iota(jnp.int32, (rows, 2 * LANES), 0)
    ev_q = jnp.where(
        row < block, order_ref[2 * me] * block + row, (order_ref[2 * me + 1] - 1) * block + row
    )
    evq_ref[...] = ev_q
    stq_ref[...] = starts(ev_q)

    zero_a = jnp.zeros_like(act_a)
    picks_low = [low & head0, low & ~head0]
    picks_high = [(~low) & head0, (~low) & ~head0]
    rolled_b = pltpu.roll(act[:, LANES:], 64, 1).astype(BF16)

    def masked(values, picks):
        return [jnp.where(pick, values, zero_a) for pick in picks]

    q_heads = masked(act_a, picks_high)
    units = jnp.where(low, act_a, zero_a).astype(F32)
    gout = gout_ref[...]
    wout_wide = jnp.concatenate([wout_ref[...], jnp.zeros_like(wout_ref[...])], axis=0)
    gated_grad = dot_nt(gout, wout_wide)
    norm_grad = gated_grad * units

    acc_ref[...] = jnp.zeros_like(acc_ref)
    key_lane = lax.broadcasted_iota(jnp.int32, (1, 2 * LANES), 1)

    def query_live(p):
        ev_j = jnp.where(
            key_lane < block,
            order_ref[2 * p] * block + key_lane,
            (order_ref[2 * p + 1] - 1) * block + key_lane,
        )
        live = (ev_j <= evq_ref[...]) & (ev_j >= stq_ref[...])
        return jnp.where(live, score_scale, 0.0)

    def forward(s, c):
        @pl.when(s > 0)
        def _():
            arrived(ctx_copy, 0, kv_all, kv_all, me, n, False, s)

        p = lax.rem(me + n - s, n)
        kv = kv_all[p]
        scale = query_live(p)
        for h in range(2):
            weights, slope = silu_parts(dot_nt(q_heads[h], kv), scale)
            if keep:
                dq_ref[p, h] = slope
            acc_ref[h] += dot_nn(weights, kv)
        return c

    lax.fori_loop(0, n, forward, 0)
    attended = jnp.where(low, jnp.where(head0, acc_ref[0], acc_ref[1]), 0.0)

    def total(v):
        return jnp.sum(v, axis=1, keepdims=True)

    cols = jnp.where(lane == 0, total(attended), 0.0)
    cols = jnp.where(lane == 1, total(attended * attended), cols)
    cols = jnp.where(lane == 2, total(norm_grad), cols)
    cols = jnp.where(lane == 3, total(norm_grad * attended), cols)
    st_all[hd] = jnp.transpose(cols)[:8]
    spread(head_copy, 0, st_all, st_all, hd, m, False)

    lane_half = lax.broadcasted_iota(jnp.int32, (1, LANES), 1)
    ev_k = evq_ref[:, :LANES]
    k_heads = [masked(rolled_b, picks_low), masked(act_b, picks_high)]
    v_heads = [masked(act_b, picks_low), masked(rolled_b, picks_high)]

    def key_parts(p, part_no):
        ev_i = order_ref[2 * p + part_no] * block + lane_half
        live = (evq_ref[:, :LANES] <= ev_i) & (evq_ref[:, :LANES] >= starts(ev_i))
        scale = jnp.where(live, score_scale, 0.0)
        q = q_all[p]
        return [silu_parts(dot_nt(k_heads[part_no][h], q), scale) for h in range(2)]

    def key_prepare(s, c):
        @pl.when(s > 0)
        def _():
            arrived(ctx_copy, 1, q_all, q_all, me, n, False, s)

        if keep:
            p = lax.rem(me + n - s, n)
            for part_no in range(2):
                for h, (weights, slope) in enumerate(key_parts(p, part_no)):
                    wk_ref[p, part_no, h] = weights
                    dk_ref[p, part_no, h] = slope
        return c

    def stats_in(s, c):
        arrived(head_copy, 0, st_all, st_all, hd, m, False, s)
        return c

    lax.fori_loop(1, m, stats_in, 0)
    stats = st_all[0]
    for i in range(1, m):
        stats = stats + st_all[i]
    stats = jnp.transpose(jnp.concatenate([stats] * 16, axis=0)) / width
    attn_mean = stats[:, 0:1]
    attn_inv = lax.rsqrt(stats[:, 1:2] - attn_mean * attn_mean + 1e-05)
    grad_mean = stats[:, 2:3]
    cross_mean = (stats[:, 3:4] - attn_mean * grad_mean) * attn_inv
    attn_norm = jnp.where(low, (attended - attn_mean) * attn_inv, 0.0)
    attn_grad = jnp.where(low, (norm_grad - grad_mean - attn_norm * cross_mean) * attn_inv, 0.0)
    ag_all[me] = jnp.where(
        low_half, attn_grad[:half], pltpu.roll(attn_grad[half:], 64, 1)
    ).astype(BF16)
    spread(ctx_copy, 2, ag_all, ag_all, me, n, False)

    units_grad = gated_grad * attn_norm
    gated = (attn_norm * units).astype(BF16)
    wo_part = dot_tn(gout, gated).astype(BF16)
    if wo_send.shape[1] != chunk:
        wo_send[...] = jnp.zeros_like(wo_send)
        uv_send[...] = jnp.zeros_like(uv_send)
    for i in range(n):
        wo_send[i, :chunk] = wo_part[i * chunk : (i + 1) * chunk]
    spread(ctx_copy, 3, wo_send, wo_recv, me, n, True)

    attn_grad = attn_grad.astype(BF16)
    ag_heads = masked(attn_grad, picks_low)
    lax.fori_loop(0, n, key_prepare, 0)
    acc_ref[...] = jnp.zeros_like(acc_ref)

    def query_back(p, c):
        kv = kv_all[p]
        if not keep:
            scale = query_live(p)
        for h in range(2):
            if keep:
                slope = dq_ref[p, h]
            else:
                _, slope = silu_parts(dot_nt(q_heads[h], kv), scale)
            score_grad = (dot_nt(ag_heads[h], kv) * slope).astype(BF16)
            acc_ref[h] += dot_nn(score_grad, kv)
        return c

    lax.fori_loop(0, n, query_back, 0)
    query_grad = jnp.where(head0, acc_ref[0], acc_ref[1])

    acck_ref[...] = jnp.zeros_like(acck_ref)
    accv_ref[...] = jnp.zeros_like(accv_ref)

    def key_back(s, c):
        @pl.when(s > 0)
        def _():
            arrived(ctx_copy, 2, ag_all, ag_all, me, n, False, s)

        p = lax.rem(me + n - s, n)
        q = q_all[p]
        ag = ag_all[p]
        for part_no in range(2):
            parts = None if keep else key_parts(p, part_no)
            for h in range(2):
                if keep:
                    weights, slope = wk_ref[p, part_no, h], dk_ref[p, part_no, h]
                else:
                    weights, slope = parts[h]
                score_grad = (dot_nt(v_heads[part_no][h], ag) * slope).astype(BF16)
                acck_ref[part_no, h] += dot_nn(score_grad, q)
                accv_ref[part_no, h] += dot_nn(weights, ag)
        return c

    lax.fori_loop(0, n, key_back, 0)

    def fold(acc, part_no):
        return jnp.where(head0, acc[part_no, 0], acc[part_no, 1])

    key_grad = pltpu.roll(fold(acck_ref, 0), 64, 1) + fold(acck_ref, 1)
    value_grad = fold(accv_ref, 0) + pltpu.roll(fold(accv_ref, 1), 64, 1)
    act_grad = jnp.concatenate(
        [jnp.where(low, units_grad, query_grad), jnp.where(low, value_grad, key_grad)], axis=1
    )
    pre = pre_ref[...]
    sig = 0.5 * jnp.tanh(0.5 * pre) + 0.5
    pre_grad = (act_grad * (sig * (1.0 + pre * (1.0 - sig)))).astype(BF16)
    input_part = dot_nt(pre_grad, w_ref[...]).astype(BF16)
    for i in range(m):
        ip_send[i] = input_part[i * part : (i + 1) * part]
    spread(head_copy, 1, ip_send, ip_recv, hd, m, True)

    scaled_in = (normed_ref[...] * gain_ref[...]).astype(BF16)
    uv_part = dot_tn(scaled_in, pre_grad).astype(BF16)
    for i in range(n):
        uv_send[i, :chunk] = uv_part[i * chunk : (i + 1) * chunk]
    spread(ctx_copy, 4, uv_send, uv_recv, me, n, True)

    def parts_in(s, summed):
        origin = arrived(head_copy, 1, ip_send, ip_recv, hd, m, True, s)
        return summed + ip_recv[origin].astype(F32)

    input_grad = lax.fori_loop(1, m, parts_in, ip_send[hd].astype(F32))
    mine = pl.ds(pl.multiple_of(hd * part, part), part)
    scaled_grad = input_grad * gain_ref[...]
    my_normed = normed_ref[mine]
    my_istd = istd_ref[mine][:, 0:1]
    mean_a = jnp.mean(scaled_grad, axis=1, keepdims=True)
    mean_b = jnp.mean(scaled_grad * my_normed, axis=1, keepdims=True)
    tg_all[hd] = (
        gout_ref[mine].astype(F32) + (scaled_grad - mean_a - my_normed * mean_b) * my_istd
    ).astype(BF16)
    spread(head_copy, 2, tg_all, tg_all, hd, m, False)

    def wo_in(s, summed):
        origin = arrived(ctx_copy, 3, wo_send, wo_recv, me, n, True, s)
        return summed + wo_recv[origin].astype(F32)

    wo_sum = lax.fori_loop(1, n, wo_in, wo_send[me].astype(F32))
    wo_ref[...] = wo_sum[:chunk]

    def uv_in(s, summed):
        origin = arrived(ctx_copy, 4, uv_send, uv_recv, me, n, True, s)
        return summed + uv_recv[origin].astype(F32)

    uv_sum = lax.fori_loop(1, n, uv_in, uv_send[me].astype(F32))
    uvqk_ref[...] = uv_sum[:chunk]

    def tokens_in(s, c):
        arrived(head_copy, 2, tg_all, tg_all, hd, m, False, s)
        return c

    lax.fori_loop(1, m, tokens_in, 0)
    for i in range(m):
        tok_ref[i * part : (i + 1) * part] = tg_all[i]

    sent(ctx_copy, 0, kv_all, kv_all, me, n, False)
    sent(ctx_copy, 1, q_all, q_all, me, n, False)
    sent(ctx_copy, 2, ag_all, ag_all, me, n, False)
    sent(ctx_copy, 3, wo_send, wo_recv, me, n, True)
    sent(ctx_copy, 4, uv_send, uv_recv, me, n, True)
    sent(head_copy, 0, st_all, st_all, hd, m, False)
    sent(head_copy, 1, ip_send, ip_recv, hd, m, True)
    sent(head_copy, 2, tg_all, tg_all, hd, m, False)


def body(tokens, in_gain, w_uvqk, w_out, grad_out, lengths, block_order):
    rows, width = tokens.shape
    n = lax.axis_size("ctx")
    m = lax.axis_size("head")
    heads_here = w_uvqk.shape[1]
    head_dim = w_uvqk.shape[2] // 4
    total = rows * n
    block = total // block_order.shape[0]
    chunk = width // n
    padded = max(chunk, 16)
    keep = n <= 16
    kept = n if keep else 1
    w_cols = (
        w_uvqk.reshape(width, heads_here, 2, 2, head_dim)
        .transpose(0, 3, 2, 1, 4)
        .reshape(width, width)
    )
    vmem = pl.BlockSpec(memory_space=pltpu.VMEM)
    smem = pl.BlockSpec(memory_space=pltpu.SMEM)
    tok, uv, wo = pl.pallas_call(
        functools.partial(
            kernel, n, m, block, lengths.shape[0], 1.0 / (total // 2), keep
        ),
        out_shape=(
            jax.ShapeDtypeStruct((rows, width), BF16),
            jax.ShapeDtypeStruct((chunk, width), F32),
            jax.ShapeDtypeStruct((chunk, LANES), F32),
        ),
        in_specs=[smem, smem] + [vmem] * 5,
        out_specs=(vmem, vmem, vmem),
        scratch_shapes=[
            pltpu.VMEM((n, rows, LANES), BF16),
            pltpu.VMEM((n, rows // 2, LANES), BF16),
            pltpu.VMEM((n, rows // 2, LANES), BF16),
            pltpu.VMEM((m, 8, rows), F32),
            pltpu.VMEM((n, padded, LANES), BF16),
            pltpu.VMEM((n, padded, LANES), BF16),
            pltpu.VMEM((n, padded, width), BF16),
            pltpu.VMEM((n, padded, width), BF16),
            pltpu.VMEM((m, rows // m, width), BF16),
            pltpu.VMEM((m, rows // m, width), BF16),
            pltpu.VMEM((m, rows // m, width), BF16),
            pltpu.VMEM((rows, width), F32),
            pltpu.VMEM((rows, LANES), F32),
            pltpu.VMEM((rows, width), F32),
            pltpu.VMEM((rows, 2 * LANES), jnp.int32),
            pltpu.VMEM((rows, 2 * LANES), jnp.int32),
            pltpu.VMEM((2, rows, LANES), F32),
            pltpu.VMEM((2, 2, rows, LANES), F32),
            pltpu.VMEM((2, 2, rows, LANES), F32),
            pltpu.VMEM((kept, 2, rows, 2 * LANES), F32),
            pltpu.VMEM((kept, 2, 2, rows, LANES), BF16),
            pltpu.VMEM((kept, 2, 2, rows, LANES), F32),
            pltpu.SemaphoreType.DMA((5, n)),
            pltpu.SemaphoreType.DMA((5, n)),
            pltpu.SemaphoreType.DMA((3, m)),
            pltpu.SemaphoreType.DMA((3, m)),
        ],
        compiler_params=pltpu.CompilerParams(
            collective_id=0, has_side_effects=True, vmem_limit_bytes=40 * 1024 * 1024
        ),
    )(lengths, block_order, tokens, in_gain.reshape(1, width), w_cols, w_out, grad_out)
    uvqk_grad = (
        uv.reshape(chunk, 2, 2, heads_here, head_dim)
        .transpose(0, 3, 2, 1, 4)
        .reshape(chunk, heads_here, 4 * head_dim)
    )
    return tok, uvqk_grad, wo[:, : heads_here * head_dim].T


def solution(mesh):
    in_specs = (
        P("ctx", None),
        P(),
        P(None, "head", None),
        P("head", None),
        P("ctx", None),
        P(),
        P(),
    )
    out_specs = (P("ctx", None), P("ctx", "head", None), P("head", "ctx"))
    return jax.shard_map(body, mesh=mesh, in_specs=in_specs, out_specs=out_specs, check_vma=False)
```

```python
import functools

import jax
import jax.numpy as jnp
from jax import lax
from jax.experimental import pallas as pl
from jax.experimental.pallas import tpu as pltpu
from jax.sharding import PartitionSpec as P

F32 = jnp.float32
BF16 = jnp.bfloat16
LANES = 128
MESH = pl.DeviceIdType.MESH


def dot_nt(a, b):
    return lax.dot_general(a, b, (((1,), (1,)), ((), ())), preferred_element_type=F32)


def dot_nn(a, b):
    return lax.dot_general(a, b, (((1,), (0,)), ((), ())), preferred_element_type=F32)


def dot_tn(a, b):
    return lax.dot_general(a, b, (((0,), (0,)), ((), ())), preferred_element_type=F32)


def silu_parts(scores, scale):
    sigma = 0.5 * jnp.tanh(0.5 * scores) + 0.5
    silu = scores * sigma
    return (silu * scale).astype(BF16), (sigma + silu * (1.0 - sigma)) * scale


def kernel(
    n, m, block, users, score_scale, keep,
    lengths_ref, order_ref, tokens_ref, gain_ref, w_ref, wout_ref, gout_ref,
    tok_ref, uvqk_ref, wo_ref,
    kv_all, q_all, ag_all, st_all, wo_send, wo_recv, uv_send, uv_recv,
    ip_send, ip_recv, tg_all, normed_ref, istd_ref, pre_ref, evq_ref, stq_ref,
    acc_ref, acck_ref, accv_ref, dq_ref, wk_ref, dk_ref,
    c_send, c_recv, h_send, h_recv,
):
    me = lax.axis_index("ctx")
    hd = lax.axis_index("head")
    rows, width = tokens_ref.shape
    half = rows // 2
    part = rows // m
    chunk = width // n

    barrier = pltpu.get_barrier_semaphore()

    def greet_ctx(s, c):
        pl.semaphore_signal(
            barrier, inc=1, device_id={"ctx": lax.rem(me + s, n)}, device_id_type=MESH
        )
        return c

    def greet_head(s, c):
        pl.semaphore_signal(
            barrier, inc=1, device_id={"head": lax.rem(hd + s, m)}, device_id_type=MESH
        )
        return c

    lax.fori_loop(1, n, greet_ctx, 0)
    lax.fori_loop(1, m, greet_head, 0)

    def ctx_copy(kind, src, dst, slot, sem, peer):
        return pltpu.make_async_remote_copy(
            src_ref=src.at[slot],
            dst_ref=dst.at[sem],
            send_sem=c_send.at[kind, slot if src is not dst else peer],
            recv_sem=c_recv.at[kind, sem],
            device_id={"ctx": peer},
            device_id_type=MESH,
        )

    def head_copy(kind, src, dst, slot, sem, peer):
        return pltpu.make_async_remote_copy(
            src_ref=src.at[slot],
            dst_ref=dst.at[sem],
            send_sem=h_send.at[kind, slot if src is not dst else peer],
            recv_sem=h_recv.at[kind, sem],
            device_id={"head": peer},
            device_id_type=MESH,
        )

    def spread(copy, kind, src, dst, mine, count, scatter):
        def step(s, c):
            peer = lax.rem(mine + s, count)
            copy(kind, src, dst, peer if scatter else mine, mine, peer).start()
            return c

        lax.fori_loop(1, count, step, 0)

    def arrived(copy, kind, src, dst, mine, count, scatter, s):
        origin = lax.rem(mine + count - s, count)
        copy(kind, src, dst, origin if scatter else mine, origin, origin).wait_recv()
        return origin

    lines = n // 2
    pair = me + 1 - 2 * lax.rem(me, 2)

    def line_origin(s):
        return lax.rem(me + n - 2 * s, n)

    def pair_origin(s):
        return lax.rem(pair + n - 2 * s, n)

    def hop(kind, buf, slot, sem, peer):
        return pltpu.make_async_remote_copy(
            src_ref=buf.at[slot],
            dst_ref=buf.at[slot],
            send_sem=c_send.at[kind, sem],
            recv_sem=c_recv.at[kind, slot],
            device_id={"ctx": peer},
            device_id_type=MESH,
        )

    def gather(kind, buf):
        def step(s, c):
            peer = lax.rem(me + 2 * s, n)
            hop(kind, buf, me, peer, peer).start()
            return c

        hop(kind, buf, me, pair, pair).start()
        lax.fori_loop(1, lines, step, 0)

    def relay(kind, buf, s):
        origin = line_origin(s)
        hop(kind, buf, origin, pair_origin(s), pair).wait_recv()
        hop(kind, buf, origin, origin + 1 - 2 * lax.rem(origin, 2), pair).start()

    def relayed(kind, buf, s):
        origin = pair_origin(s)
        hop(kind, buf, origin, origin, pair).wait_recv()

    def sent(copy, kind, src, dst, mine, count, scatter):
        def step(s, c):
            peer = lax.rem(mine + s, count)
            copy(kind, src, dst, peer if scatter else mine, mine, peer).wait_send()
            return c

        lax.fori_loop(1, count, step, 0)

    x = tokens_ref[...].astype(F32)
    centered = x - jnp.mean(x, axis=1, keepdims=True)
    istd = lax.rsqrt(jnp.mean(centered * centered, axis=1, keepdims=True) + 1e-05)
    normed = centered * istd
    normed_ref[...] = normed
    istd_ref[...] = jnp.broadcast_to(istd, (rows, LANES))
    scaled_in = (normed * gain_ref[...]).astype(BF16)

    def project(cols):
        pre = dot_nn(scaled_in, w_ref[:, cols])
        pre_ref[:, cols] = pre
        return pre * (0.5 * jnp.tanh(0.5 * pre) + 0.5)

    wide_b = project(slice(LANES, 2 * LANES))
    act_b = wide_b.astype(BF16)
    kv_all[me] = act_b
    pl.semaphore_wait(barrier, n + m - 2)
    gather(0, kv_all)
    wide_a = project(slice(0, LANES))
    act_a = wide_a.astype(BF16)
    lane = lax.broadcasted_iota(jnp.int32, (rows, LANES), 1)
    low = lane < 64
    head0 = (lane & 32) == 0
    low_half = lax.broadcasted_iota(jnp.int32, (half, LANES), 1) < 64
    q_all[me] = jnp.where(
        low_half, pltpu.roll(wide_a[:half], 64, 1), wide_a[half:]
    ).astype(BF16)

    gather(1, q_all)

    ends = []
    running = jnp.int32(0)
    for u in range(users):
        running = running + lengths_ref[u]
        ends.append(running)

    def starts(events):
        begin = jnp.zeros_like(events)
        for end in ends:
            begin = jnp.where(events >= end, end, begin)
        return begin

    row = lax.broadcasted_iota(jnp.int32, (rows, 2 * LANES), 0)
    ev_q = jnp.where(
        row < block, order_ref[2 * me] * block + row, (order_ref[2 * me + 1] - 1) * block + row
    )
    evq_ref[...] = ev_q
    stq_ref[...] = starts(ev_q)

    zero_a = jnp.zeros_like(act_a)
    picks_low = [low & head0, low & ~head0]
    picks_high = [(~low) & head0, (~low) & ~head0]
    rolled_b = pltpu.roll(wide_b, 64, 1).astype(BF16)

    def masked(values, picks):
        return [jnp.where(pick, values, zero_a) for pick in picks]

    q_heads = masked(act_a, picks_high)
    units = jnp.where(low, act_a, zero_a).astype(F32)
    gout = gout_ref[...]
    wout_wide = jnp.concatenate([wout_ref[...], jnp.zeros_like(wout_ref[...])], axis=0)
    gated_grad = dot_nt(gout, wout_wide)
    norm_grad = gated_grad * units

    acc_ref[...] = jnp.zeros_like(acc_ref)
    key_lane = lax.broadcasted_iota(jnp.int32, (1, 2 * LANES), 1)

    def query_live(p):
        ev_j = jnp.where(
            key_lane < block,
            order_ref[2 * p] * block + key_lane,
            (order_ref[2 * p + 1] - 1) * block + key_lane,
        )
        live = (ev_j <= evq_ref[...]) & (ev_j >= stq_ref[...])
        return jnp.where(live, score_scale, 0.0)

    def forward(p):
        kv = kv_all[p]
        scale = query_live(p)
        for h in range(2):
            weights, slope = silu_parts(dot_nt(q_heads[h], kv), scale)
            if keep:
                dq_ref[p, h] = slope
            acc_ref[h] += dot_nn(weights, kv)

    def forward_step(s, c):
        @pl.when(s < lines)
        def _():
            @pl.when(s > 0)
            def _():
                relay(0, kv_all, s)

            forward(line_origin(s))

        @pl.when(s > 0)
        def _():
            relayed(0, kv_all, s - 1)
            forward(pair_origin(s - 1))

        return c

    lax.fori_loop(0, lines + 1, forward_step, 0)
    attended = jnp.where(low, jnp.where(head0, acc_ref[0], acc_ref[1]), 0.0)

    def total(v):
        return jnp.sum(v, axis=1, keepdims=True)

    cols = jnp.where(lane == 0, total(attended), 0.0)
    cols = jnp.where(lane == 1, total(attended * attended), cols)
    cols = jnp.where(lane == 2, total(norm_grad), cols)
    cols = jnp.where(lane == 3, total(norm_grad * attended), cols)
    st_all[hd] = jnp.transpose(cols)[:8]
    spread(head_copy, 0, st_all, st_all, hd, m, False)

    lane_half = lax.broadcasted_iota(jnp.int32, (1, LANES), 1)
    ev_k = evq_ref[:, :LANES]
    k_heads = [masked(rolled_b, picks_low), masked(act_b, picks_high)]
    v_heads = [masked(act_b, picks_low), masked(rolled_b, picks_high)]

    def key_parts(p, part_no):
        ev_i = order_ref[2 * p + part_no] * block + lane_half
        live = (evq_ref[:, :LANES] <= ev_i) & (evq_ref[:, :LANES] >= starts(ev_i))
        scale = jnp.where(live, score_scale, 0.0)
        q = q_all[p]
        return [silu_parts(dot_nt(k_heads[part_no][h], q), scale) for h in range(2)]

    def key_prepare(p):
        if keep:
            for part_no in range(2):
                for h, (weights, slope) in enumerate(key_parts(p, part_no)):
                    wk_ref[p, part_no, h] = weights
                    dk_ref[p, part_no, h] = slope

    def relay_queries(s, c):
        relay(1, q_all, s)
        return c

    def prepare_line(s, c):
        key_prepare(line_origin(s))
        return c

    def prepare_pair(s, c):
        relayed(1, q_all, s)
        key_prepare(pair_origin(s))
        return c

    lax.fori_loop(1, lines, relay_queries, 0)
    lax.fori_loop(0, lines, prepare_line, 0)

    def stats_in(s, c):
        arrived(head_copy, 0, st_all, st_all, hd, m, False, s)
        return c

    lax.fori_loop(1, m, stats_in, 0)
    stats = st_all[0]
    for i in range(1, m):
        stats = stats + st_all[i]
    stats = jnp.transpose(jnp.concatenate([stats] * 16, axis=0)) / width
    attn_mean = stats[:, 0:1]
    attn_inv = lax.rsqrt(stats[:, 1:2] - attn_mean * attn_mean + 1e-05)
    grad_mean = stats[:, 2:3]
    cross_mean = (stats[:, 3:4] - attn_mean * grad_mean) * attn_inv
    attn_norm = jnp.where(low, (attended - attn_mean) * attn_inv, 0.0)
    attn_grad = jnp.where(low, (norm_grad - grad_mean - attn_norm * cross_mean) * attn_inv, 0.0)
    ag_all[me] = jnp.where(
        low_half, attn_grad[:half], pltpu.roll(attn_grad[half:], 64, 1)
    ).astype(BF16)
    gather(2, ag_all)

    units_grad = gated_grad * attn_norm
    gated = (attn_norm * units).astype(BF16)
    wo_part = dot_tn(gout, gated).astype(BF16)
    if wo_send.shape[1] != chunk:
        wo_send[...] = jnp.zeros_like(wo_send)
        uv_send[...] = jnp.zeros_like(uv_send)
    for i in range(n):
        wo_send[i, :chunk] = wo_part[i * chunk : (i + 1) * chunk]
    spread(ctx_copy, 3, wo_send, wo_recv, me, n, True)

    attn_grad = attn_grad.astype(BF16)
    ag_heads = masked(attn_grad, picks_low)
    lax.fori_loop(0, lines, prepare_pair, 0)

    def relay_grads(s, c):
        relay(2, ag_all, s)
        return c

    lax.fori_loop(1, lines, relay_grads, 0)
    acc_ref[...] = jnp.zeros_like(acc_ref)

    def query_back(p, c):
        kv = kv_all[p]
        if not keep:
            scale = query_live(p)
        for h in range(2):
            if keep:
                slope = dq_ref[p, h]
            else:
                _, slope = silu_parts(dot_nt(q_heads[h], kv), scale)
            score_grad = (dot_nt(ag_heads[h], kv) * slope).astype(BF16)
            acc_ref[h] += dot_nn(score_grad, kv)
        return c

    lax.fori_loop(0, n, query_back, 0)
    query_grad = jnp.where(head0, acc_ref[0], acc_ref[1])

    acck_ref[...] = jnp.zeros_like(acck_ref)
    accv_ref[...] = jnp.zeros_like(accv_ref)

    def key_back(p):
        q = q_all[p]
        ag = ag_all[p]
        for part_no in range(2):
            parts = None if keep else key_parts(p, part_no)
            for h in range(2):
                if keep:
                    weights, slope = wk_ref[p, part_no, h], dk_ref[p, part_no, h]
                else:
                    weights, slope = parts[h]
                score_grad = (dot_nt(v_heads[part_no][h], ag) * slope).astype(BF16)
                acck_ref[part_no, h] += dot_nn(score_grad, q)
                accv_ref[part_no, h] += dot_nn(weights, ag)

    def line_back(s, c):
        key_back(line_origin(s))
        return c

    def pair_back(s, c):
        relayed(2, ag_all, s)
        key_back(pair_origin(s))
        return c

    lax.fori_loop(0, lines, line_back, 0)
    lax.fori_loop(0, lines, pair_back, 0)

    def fold(acc, part_no):
        return jnp.where(head0, acc[part_no, 0], acc[part_no, 1])

    key_grad = pltpu.roll(fold(acck_ref, 0), 64, 1) + fold(acck_ref, 1)
    value_grad = fold(accv_ref, 0) + pltpu.roll(fold(accv_ref, 1), 64, 1)
    act_grad = jnp.concatenate(
        [jnp.where(low, units_grad, query_grad), jnp.where(low, value_grad, key_grad)], axis=1
    )
    pre = pre_ref[...]
    sig = 0.5 * jnp.tanh(0.5 * pre) + 0.5
    pre_grad = (act_grad * (sig * (1.0 + pre * (1.0 - sig)))).astype(BF16)
    input_part = dot_nt(pre_grad, w_ref[...]).astype(BF16)
    for i in range(m):
        ip_send[i] = input_part[i * part : (i + 1) * part]
    spread(head_copy, 1, ip_send, ip_recv, hd, m, True)

    scaled_in = (normed_ref[...] * gain_ref[...]).astype(BF16)
    uv_part = dot_tn(scaled_in, pre_grad).astype(BF16)
    for i in range(n):
        uv_send[i, :chunk] = uv_part[i * chunk : (i + 1) * chunk]
    spread(ctx_copy, 4, uv_send, uv_recv, me, n, True)

    def parts_in(s, summed):
        origin = arrived(head_copy, 1, ip_send, ip_recv, hd, m, True, s)
        return summed + ip_recv[origin].astype(F32)

    input_grad = lax.fori_loop(1, m, parts_in, ip_send[hd].astype(F32))
    mine = pl.ds(pl.multiple_of(hd * part, part), part)
    scaled_grad = input_grad * gain_ref[...]
    my_normed = normed_ref[mine]
    my_istd = istd_ref[mine][:, 0:1]
    mean_a = jnp.mean(scaled_grad, axis=1, keepdims=True)
    mean_b = jnp.mean(scaled_grad * my_normed, axis=1, keepdims=True)
    tg_all[hd] = (
        gout_ref[mine].astype(F32) + (scaled_grad - mean_a - my_normed * mean_b) * my_istd
    ).astype(BF16)
    spread(head_copy, 2, tg_all, tg_all, hd, m, False)

    def wo_in(s, summed):
        origin = arrived(ctx_copy, 3, wo_send, wo_recv, me, n, True, s)
        return summed + wo_recv[origin].astype(F32)

    wo_sum = lax.fori_loop(1, n, wo_in, wo_send[me].astype(F32))
    wo_ref[...] = wo_sum[:chunk]

    def uv_in(s, summed):
        origin = arrived(ctx_copy, 4, uv_send, uv_recv, me, n, True, s)
        return summed + uv_recv[origin].astype(F32)

    uv_sum = lax.fori_loop(1, n, uv_in, uv_send[me].astype(F32))
    uvqk_ref[...] = uv_sum[:chunk]

    def tokens_in(s, c):
        arrived(head_copy, 2, tg_all, tg_all, hd, m, False, s)
        return c

    lax.fori_loop(1, m, tokens_in, 0)
    for i in range(m):
        tok_ref[i * part : (i + 1) * part] = tg_all[i]

    sent(ctx_copy, 0, kv_all, kv_all, me, n, False)
    sent(ctx_copy, 1, q_all, q_all, me, n, False)
    sent(ctx_copy, 2, ag_all, ag_all, me, n, False)
    sent(ctx_copy, 3, wo_send, wo_recv, me, n, True)
    sent(ctx_copy, 4, uv_send, uv_recv, me, n, True)
    sent(head_copy, 0, st_all, st_all, hd, m, False)
    sent(head_copy, 1, ip_send, ip_recv, hd, m, True)
    sent(head_copy, 2, tg_all, tg_all, hd, m, False)


def body(tokens, in_gain, w_uvqk, w_out, grad_out, lengths, block_order):
    rows, width = tokens.shape
    n = lax.axis_size("ctx")
    m = lax.axis_size("head")
    heads_here = w_uvqk.shape[1]
    head_dim = w_uvqk.shape[2] // 4
    total = rows * n
    block = total // block_order.shape[0]
    chunk = width // n
    padded = max(chunk, 16)
    keep = n <= 16
    kept = n if keep else 1
    w_cols = (
        w_uvqk.reshape(width, heads_here, 2, 2, head_dim)
        .transpose(0, 3, 2, 1, 4)
        .reshape(width, width)
    )
    vmem = pl.BlockSpec(memory_space=pltpu.VMEM)
    smem = pl.BlockSpec(memory_space=pltpu.SMEM)
    tok, uv, wo = pl.pallas_call(
        functools.partial(
            kernel, n, m, block, lengths.shape[0], 1.0 / (total // 2), keep
        ),
        out_shape=(
            jax.ShapeDtypeStruct((rows, width), BF16),
            jax.ShapeDtypeStruct((chunk, width), F32),
            jax.ShapeDtypeStruct((chunk, LANES), F32),
        ),
        in_specs=[smem, smem] + [vmem] * 5,
        out_specs=(vmem, vmem, vmem),
        scratch_shapes=[
            pltpu.VMEM((n, rows, LANES), BF16),
            pltpu.VMEM((n, rows // 2, LANES), BF16),
            pltpu.VMEM((n, rows // 2, LANES), BF16),
            pltpu.VMEM((m, 8, rows), F32),
            pltpu.VMEM((n, padded, LANES), BF16),
            pltpu.VMEM((n, padded, LANES), BF16),
            pltpu.VMEM((n, padded, width), BF16),
            pltpu.VMEM((n, padded, width), BF16),
            pltpu.VMEM((m, rows // m, width), BF16),
            pltpu.VMEM((m, rows // m, width), BF16),
            pltpu.VMEM((m, rows // m, width), BF16),
            pltpu.VMEM((rows, width), F32),
            pltpu.VMEM((rows, LANES), F32),
            pltpu.VMEM((rows, width), F32),
            pltpu.VMEM((rows, 2 * LANES), jnp.int32),
            pltpu.VMEM((rows, 2 * LANES), jnp.int32),
            pltpu.VMEM((2, rows, LANES), F32),
            pltpu.VMEM((2, 2, rows, LANES), F32),
            pltpu.VMEM((2, 2, rows, LANES), F32),
            pltpu.VMEM((kept, 2, rows, 2 * LANES), F32),
            pltpu.VMEM((kept, 2, 2, rows, LANES), BF16),
            pltpu.VMEM((kept, 2, 2, rows, LANES), F32),
            pltpu.SemaphoreType.DMA((5, n)),
            pltpu.SemaphoreType.DMA((5, n)),
            pltpu.SemaphoreType.DMA((3, m)),
            pltpu.SemaphoreType.DMA((3, m)),
        ],
        compiler_params=pltpu.CompilerParams(
            collective_id=0, has_side_effects=True, vmem_limit_bytes=40 * 1024 * 1024
        ),
    )(lengths, block_order, tokens, in_gain.reshape(1, width), w_cols, w_out, grad_out)
    uvqk_grad = (
        uv.reshape(chunk, 2, 2, heads_here, head_dim)
        .transpose(0, 3, 2, 1, 4)
        .reshape(chunk, heads_here, 4 * head_dim)
    )
    return tok, uvqk_grad, wo[:, : heads_here * head_dim].T


def solution(mesh):
    in_specs = (
        P("ctx", None),
        P(),
        P(None, "head", None),
        P("head", None),
        P("ctx", None),
        P(),
        P(),
    )
    out_specs = (P("ctx", None), P("ctx", "head", None), P("head", "ctx"))
    return jax.shard_map(body, mesh=mesh, in_specs=in_specs, out_specs=out_specs, check_vma=False)
```

```python
import functools

import jax
import jax.numpy as jnp
from jax import lax
from jax.experimental import pallas as pl
from jax.experimental.pallas import tpu as pltpu
from jax.sharding import PartitionSpec as P

F32 = jnp.float32
BF16 = jnp.bfloat16
LANES = 128
MESH = pl.DeviceIdType.MESH


def dot_nt(a, b):
    return lax.dot_general(a, b, (((1,), (1,)), ((), ())), preferred_element_type=F32)


def dot_nn(a, b):
    return lax.dot_general(a, b, (((1,), (0,)), ((), ())), preferred_element_type=F32)


def dot_tn(a, b):
    return lax.dot_general(a, b, (((0,), (0,)), ((), ())), preferred_element_type=F32)


def silu_parts(scores, scale):
    sigma = 0.5 * jnp.tanh(0.5 * scores) + 0.5
    silu = scores * sigma
    return (silu * scale).astype(BF16), (sigma + silu * (1.0 - sigma)) * scale


def kernel(
    n, m, block, users, score_scale, keep,
    lengths_ref, order_ref, tokens_ref, gain_ref, w_ref, wout_ref, gout_ref,
    tok_ref, uvqk_ref, wo_ref,
    kv_all, q_all, ag_all, st_all, wo_send, wo_recv, uv_send, uv_recv,
    ip_send, ip_recv, tg_all, normed_ref, istd_ref, pre_ref, evq_ref, stq_ref,
    acc_ref, acck_ref, accv_ref, dq_ref, wk_ref, dk_ref,
    c_send, c_recv, h_send, h_recv,
):
    me = lax.axis_index("ctx")
    hd = lax.axis_index("head")
    rows, width = tokens_ref.shape
    half = rows // 2
    part = rows // m
    chunk = width // n

    barrier = pltpu.get_barrier_semaphore()

    def greet_ctx(s, c):
        pl.semaphore_signal(
            barrier, inc=1, device_id={"ctx": lax.rem(me + s, n)}, device_id_type=MESH
        )
        return c

    def greet_head(s, c):
        pl.semaphore_signal(
            barrier, inc=1, device_id={"head": lax.rem(hd + s, m)}, device_id_type=MESH
        )
        return c

    lax.fori_loop(1, n, greet_ctx, 0, unroll=keep)
    lax.fori_loop(1, m, greet_head, 0, unroll=keep)

    def ctx_copy(kind, src, dst, slot, sem, peer):
        return pltpu.make_async_remote_copy(
            src_ref=src.at[slot],
            dst_ref=dst.at[sem],
            send_sem=c_send.at[kind, slot if src is not dst else peer],
            recv_sem=c_recv.at[kind, sem],
            device_id={"ctx": peer},
            device_id_type=MESH,
        )

    def head_copy(kind, src, dst, slot, sem, peer):
        return pltpu.make_async_remote_copy(
            src_ref=src.at[slot],
            dst_ref=dst.at[sem],
            send_sem=h_send.at[kind, slot if src is not dst else peer],
            recv_sem=h_recv.at[kind, sem],
            device_id={"head": peer},
            device_id_type=MESH,
        )

    def spread(copy, kind, src, dst, mine, count, scatter):
        def step(s, c):
            peer = lax.rem(mine + s, count)
            copy(kind, src, dst, peer if scatter else mine, mine, peer).start()
            return c

        lax.fori_loop(1, count, step, 0, unroll=keep)

    def arrived(copy, kind, src, dst, mine, count, scatter, s):
        origin = lax.rem(mine + count - s, count)
        copy(kind, src, dst, origin if scatter else mine, origin, origin).wait_recv()
        return origin

    lines = n // 2
    pair = me + 1 - 2 * lax.rem(me, 2)

    def line_origin(s):
        return lax.rem(me + n - 2 * s, n)

    def pair_origin(s):
        return lax.rem(pair + n - 2 * s, n)

    def hop(kind, buf, slot, sem, peer):
        return pltpu.make_async_remote_copy(
            src_ref=buf.at[slot],
            dst_ref=buf.at[slot],
            send_sem=c_send.at[kind, sem],
            recv_sem=c_recv.at[kind, slot],
            device_id={"ctx": peer},
            device_id_type=MESH,
        )

    def gather(kind, buf):
        def step(s, c):
            peer = lax.rem(me + 2 * s, n)
            hop(kind, buf, me, peer, peer).start()
            return c

        hop(kind, buf, me, pair, pair).start()
        lax.fori_loop(1, lines, step, 0, unroll=keep)

    def relay(kind, buf, s):
        origin = line_origin(s)
        hop(kind, buf, origin, pair_origin(s), pair).wait_recv()
        hop(kind, buf, origin, origin + 1 - 2 * lax.rem(origin, 2), pair).start()

    def relayed(kind, buf, s):
        origin = pair_origin(s)
        hop(kind, buf, origin, origin, pair).wait_recv()

    def sent(copy, kind, src, dst, mine, count, scatter):
        def step(s, c):
            peer = lax.rem(mine + s, count)
            copy(kind, src, dst, peer if scatter else mine, mine, peer).wait_send()
            return c

        lax.fori_loop(1, count, step, 0, unroll=keep)

    x = tokens_ref[...].astype(F32)
    centered = x - jnp.mean(x, axis=1, keepdims=True)
    istd = lax.rsqrt(jnp.mean(centered * centered, axis=1, keepdims=True) + 1e-05)
    normed = centered * istd
    normed_ref[...] = normed
    istd_ref[...] = jnp.broadcast_to(istd, (rows, LANES))
    scaled_in = (normed * gain_ref[...]).astype(BF16)

    def project(cols):
        pre = dot_nn(scaled_in, w_ref[:, cols])
        pre_ref[:, cols] = pre
        return pre * (0.5 * jnp.tanh(0.5 * pre) + 0.5)

    wide_b = project(slice(LANES, 2 * LANES))
    act_b = wide_b.astype(BF16)
    kv_all[me] = act_b
    pl.semaphore_wait(barrier, n + m - 2)
    gather(0, kv_all)
    wide_a = project(slice(0, LANES))
    act_a = wide_a.astype(BF16)
    lane = lax.broadcasted_iota(jnp.int32, (rows, LANES), 1)
    low = lane < 64
    head0 = (lane & 32) == 0
    low_half = lax.broadcasted_iota(jnp.int32, (half, LANES), 1) < 64
    q_all[me] = jnp.where(
        low_half, pltpu.roll(wide_a[:half], 64, 1), wide_a[half:]
    ).astype(BF16)

    gather(1, q_all)

    ends = []
    running = jnp.int32(0)
    for u in range(users):
        running = running + lengths_ref[u]
        ends.append(running)

    def starts(events):
        begin = jnp.zeros_like(events)
        for end in ends:
            begin = jnp.where(events >= end, end, begin)
        return begin

    row = lax.broadcasted_iota(jnp.int32, (rows, 2 * LANES), 0)
    ev_q = jnp.where(
        row < block, order_ref[2 * me] * block + row, (order_ref[2 * me + 1] - 1) * block + row
    )
    evq_ref[...] = ev_q
    stq_ref[...] = starts(ev_q)

    zero_a = jnp.zeros_like(act_a)
    picks_low = [low & head0, low & ~head0]
    picks_high = [(~low) & head0, (~low) & ~head0]
    rolled_b = pltpu.roll(wide_b, 64, 1).astype(BF16)

    def masked(values, picks):
        return [jnp.where(pick, values, zero_a) for pick in picks]

    q_heads = masked(act_a, picks_high)
    units = jnp.where(low, act_a, zero_a).astype(F32)
    gout = gout_ref[...]
    wout_wide = jnp.concatenate([wout_ref[...], jnp.zeros_like(wout_ref[...])], axis=0)
    gated_grad = dot_nt(gout, wout_wide)
    norm_grad = gated_grad * units

    acc_ref[...] = jnp.zeros_like(acc_ref)
    key_lane = lax.broadcasted_iota(jnp.int32, (1, 2 * LANES), 1)

    def query_live(p):
        ev_j = jnp.where(
            key_lane < block,
            order_ref[2 * p] * block + key_lane,
            (order_ref[2 * p + 1] - 1) * block + key_lane,
        )
        live = (ev_j <= evq_ref[...]) & (ev_j >= stq_ref[...])
        return jnp.where(live, score_scale, 0.0)

    def forward(p):
        kv = kv_all[p]
        scale = query_live(p)
        for h in range(2):
            weights, slope = silu_parts(dot_nt(q_heads[h], kv), scale)
            if keep:
                dq_ref[p, h] = slope
            acc_ref[h] += dot_nn(weights, kv)

    lane_half = lax.broadcasted_iota(jnp.int32, (1, LANES), 1)
    k_heads = [masked(rolled_b, picks_low), masked(act_b, picks_high)]
    v_heads = [masked(act_b, picks_low), masked(rolled_b, picks_high)]

    def key_parts(p, part_no):
        ev_i = order_ref[2 * p + part_no] * block + lane_half
        live = (evq_ref[:, :LANES] <= ev_i) & (evq_ref[:, :LANES] >= starts(ev_i))
        scale = jnp.where(live, score_scale, 0.0)
        q = q_all[p]
        return [silu_parts(dot_nt(k_heads[part_no][h], q), scale) for h in range(2)]

    def key_prepare(p):
        if keep:
            for part_no in range(2):
                for h, (weights, slope) in enumerate(key_parts(p, part_no)):
                    wk_ref[p, part_no, h] = weights
                    dk_ref[p, part_no, h] = slope

    def line_step(s, c):
        relay(0, kv_all, s)
        forward(line_origin(s))
        return c

    def pair_step(s, c):
        @pl.when(s > 0)
        def _():
            relay(1, q_all, s)

        key_prepare(line_origin(s))
        relayed(0, kv_all, s)
        forward(pair_origin(s))
        return c

    forward(me)
    lax.fori_loop(1, lines, line_step, 0, unroll=keep)
    lax.fori_loop(0, lines, pair_step, 0, unroll=keep)
    attended = jnp.where(low, jnp.where(head0, acc_ref[0], acc_ref[1]), 0.0)

    def total(v):
        return jnp.sum(v, axis=1, keepdims=True)

    cols = jnp.where(lane == 0, total(attended), 0.0)
    cols = jnp.where(lane == 1, total(attended * attended), cols)
    cols = jnp.where(lane == 2, total(norm_grad), cols)
    cols = jnp.where(lane == 3, total(norm_grad * attended), cols)
    st_all[hd] = jnp.transpose(cols)[:8]
    spread(head_copy, 0, st_all, st_all, hd, m, False)

    def prepare_pair(s, c):
        relayed(1, q_all, s)
        key_prepare(pair_origin(s))
        return c

    early = lines // 2
    lax.fori_loop(0, early, prepare_pair, 0, unroll=keep)

    def stats_in(s, c):
        arrived(head_copy, 0, st_all, st_all, hd, m, False, s)
        return c

    lax.fori_loop(1, m, stats_in, 0, unroll=keep)
    stats = st_all[0]
    for i in range(1, m):
        stats = stats + st_all[i]
    stats = jnp.transpose(jnp.concatenate([stats] * 16, axis=0)) / width
    attn_mean = stats[:, 0:1]
    attn_inv = lax.rsqrt(stats[:, 1:2] - attn_mean * attn_mean + 1e-05)
    grad_mean = stats[:, 2:3]
    cross_mean = (stats[:, 3:4] - attn_mean * grad_mean) * attn_inv
    attn_norm = jnp.where(low, (attended - attn_mean) * attn_inv, 0.0)
    attn_grad = jnp.where(low, (norm_grad - grad_mean - attn_norm * cross_mean) * attn_inv, 0.0)
    ag_all[me] = jnp.where(
        low_half, attn_grad[:half], pltpu.roll(attn_grad[half:], 64, 1)
    ).astype(BF16)
    gather(2, ag_all)

    units_grad = gated_grad * attn_norm
    gated = (attn_norm * units).astype(BF16)
    wo_part = dot_tn(gout, gated).astype(BF16)
    if wo_send.shape[1] != chunk:
        wo_send[...] = jnp.zeros_like(wo_send)
        uv_send[...] = jnp.zeros_like(uv_send)
    for i in range(n):
        wo_send[i, :chunk] = wo_part[i * chunk : (i + 1) * chunk]
    spread(ctx_copy, 3, wo_send, wo_recv, me, n, True)

    attn_grad = attn_grad.astype(BF16)
    ag_heads = masked(attn_grad, picks_low)
    lax.fori_loop(early, lines, prepare_pair, 0, unroll=keep)

    def relay_grads(s, c):
        relay(2, ag_all, s)
        return c

    lax.fori_loop(1, lines, relay_grads, 0, unroll=keep)
    acc_ref[...] = jnp.zeros_like(acc_ref)

    def query_back(i, c):
        kv = kv_all[pl.ds(2 * i, 2)].reshape(2 * rows, LANES)
        for h in range(2):
            raw = dot_nt(ag_heads[h], kv)
            grads = []
            for b in range(2):
                if keep:
                    slope = dq_ref[2 * i + b, h]
                else:
                    block_kv = kv[b * rows : (b + 1) * rows]
                    _, slope = silu_parts(dot_nt(q_heads[h], block_kv), query_live(2 * i + b))
                grads.append((raw[:, b * rows : (b + 1) * rows] * slope).astype(BF16))
            acc_ref[h] += dot_nn(jnp.concatenate(grads, axis=1), kv)
        return c

    lax.fori_loop(0, lines, query_back, 0, unroll=keep)
    query_grad = jnp.where(head0, acc_ref[0], acc_ref[1])

    acck_ref[...] = jnp.zeros_like(acck_ref)
    accv_ref[...] = jnp.zeros_like(accv_ref)

    def key_back(p):
        q = q_all[p]
        ag = ag_all[p]
        for part_no in range(2):
            parts = None if keep else key_parts(p, part_no)
            for h in range(2):
                if keep:
                    weights, slope = wk_ref[p, part_no, h], dk_ref[p, part_no, h]
                else:
                    weights, slope = parts[h]
                score_grad = (dot_nt(v_heads[part_no][h], ag) * slope).astype(BF16)
                acck_ref[part_no, h] += dot_nn(score_grad, q)
                accv_ref[part_no, h] += dot_nn(weights, ag)

    def line_back(s, c):
        key_back(line_origin(s))
        return c

    def pair_back(s, c):
        relayed(2, ag_all, s)
        key_back(pair_origin(s))
        return c

    lax.fori_loop(0, lines, line_back, 0, unroll=keep)
    lax.fori_loop(0, lines, pair_back, 0, unroll=keep)

    def fold(acc, part_no):
        return jnp.where(head0, acc[part_no, 0], acc[part_no, 1])

    key_grad = pltpu.roll(fold(acck_ref, 0), 64, 1) + fold(acck_ref, 1)
    value_grad = fold(accv_ref, 0) + pltpu.roll(fold(accv_ref, 1), 64, 1)
    act_grad = jnp.concatenate(
        [jnp.where(low, units_grad, query_grad), jnp.where(low, value_grad, key_grad)], axis=1
    )
    pre = pre_ref[...]
    sig = 0.5 * jnp.tanh(0.5 * pre) + 0.5
    pre_grad = (act_grad * (sig * (1.0 + pre * (1.0 - sig)))).astype(BF16)
    input_part = dot_nt(pre_grad, w_ref[...]).astype(BF16)
    for i in range(m):
        ip_send[i] = input_part[i * part : (i + 1) * part]
    spread(head_copy, 1, ip_send, ip_recv, hd, m, True)

    scaled_in = (normed_ref[...] * gain_ref[...]).astype(BF16)
    uv_part = dot_tn(scaled_in, pre_grad).astype(BF16)
    for i in range(n):
        uv_send[i, :chunk] = uv_part[i * chunk : (i + 1) * chunk]
    spread(ctx_copy, 4, uv_send, uv_recv, me, n, True)

    def parts_in(s, summed):
        origin = arrived(head_copy, 1, ip_send, ip_recv, hd, m, True, s)
        return summed + ip_recv[origin].astype(F32)

    input_grad = lax.fori_loop(1, m, parts_in, ip_send[hd].astype(F32), unroll=keep)
    mine = pl.ds(pl.multiple_of(hd * part, part), part)
    scaled_grad = input_grad * gain_ref[...]
    my_normed = normed_ref[mine]
    my_istd = istd_ref[mine][:, 0:1]
    mean_a = jnp.mean(scaled_grad, axis=1, keepdims=True)
    mean_b = jnp.mean(scaled_grad * my_normed, axis=1, keepdims=True)
    tg_all[hd] = (
        gout_ref[mine].astype(F32) + (scaled_grad - mean_a - my_normed * mean_b) * my_istd
    ).astype(BF16)
    spread(head_copy, 2, tg_all, tg_all, hd, m, False)

    def wo_in(s, summed):
        origin = arrived(ctx_copy, 3, wo_send, wo_recv, me, n, True, s)
        return summed + wo_recv[origin].astype(F32)

    wo_sum = lax.fori_loop(1, n, wo_in, wo_send[me].astype(F32), unroll=keep)
    wo_ref[...] = wo_sum[:chunk]

    def uv_in(s, summed):
        origin = arrived(ctx_copy, 4, uv_send, uv_recv, me, n, True, s)
        return summed + uv_recv[origin].astype(F32)

    uv_sum = lax.fori_loop(1, n, uv_in, uv_send[me].astype(F32), unroll=keep)
    uvqk_ref[...] = uv_sum[:chunk]

    def tokens_in(s, c):
        arrived(head_copy, 2, tg_all, tg_all, hd, m, False, s)
        return c

    lax.fori_loop(1, m, tokens_in, 0, unroll=keep)
    for i in range(m):
        tok_ref[i * part : (i + 1) * part] = tg_all[i]

    sent(ctx_copy, 0, kv_all, kv_all, me, n, False)
    sent(ctx_copy, 1, q_all, q_all, me, n, False)
    sent(ctx_copy, 2, ag_all, ag_all, me, n, False)
    sent(ctx_copy, 3, wo_send, wo_recv, me, n, True)
    sent(ctx_copy, 4, uv_send, uv_recv, me, n, True)
    sent(head_copy, 0, st_all, st_all, hd, m, False)
    sent(head_copy, 1, ip_send, ip_recv, hd, m, True)
    sent(head_copy, 2, tg_all, tg_all, hd, m, False)


def body(tokens, in_gain, w_uvqk, w_out, grad_out, lengths, block_order):
    rows, width = tokens.shape
    n = lax.axis_size("ctx")
    m = lax.axis_size("head")
    heads_here = w_uvqk.shape[1]
    head_dim = w_uvqk.shape[2] // 4
    total = rows * n
    block = total // block_order.shape[0]
    chunk = width // n
    padded = max(chunk, 16)
    keep = n <= 16
    kept = n if keep else 1
    w_cols = (
        w_uvqk.reshape(width, heads_here, 2, 2, head_dim)
        .transpose(0, 3, 2, 1, 4)
        .reshape(width, width)
    )
    vmem = pl.BlockSpec(memory_space=pltpu.VMEM)
    smem = pl.BlockSpec(memory_space=pltpu.SMEM)
    tok, uv, wo = pl.pallas_call(
        functools.partial(
            kernel, n, m, block, lengths.shape[0], 1.0 / (total // 2), keep
        ),
        out_shape=(
            jax.ShapeDtypeStruct((rows, width), BF16),
            jax.ShapeDtypeStruct((chunk, width), F32),
            jax.ShapeDtypeStruct((chunk, LANES), F32),
        ),
        in_specs=[smem, smem] + [vmem] * 5,
        out_specs=(vmem, vmem, vmem),
        scratch_shapes=[
            pltpu.VMEM((n, rows, LANES), BF16),
            pltpu.VMEM((n, rows // 2, LANES), BF16),
            pltpu.VMEM((n, rows // 2, LANES), BF16),
            pltpu.VMEM((m, 8, rows), F32),
            pltpu.VMEM((n, padded, LANES), BF16),
            pltpu.VMEM((n, padded, LANES), BF16),
            pltpu.VMEM((n, padded, width), BF16),
            pltpu.VMEM((n, padded, width), BF16),
            pltpu.VMEM((m, rows // m, width), BF16),
            pltpu.VMEM((m, rows // m, width), BF16),
            pltpu.VMEM((m, rows // m, width), BF16),
            pltpu.VMEM((rows, width), F32),
            pltpu.VMEM((rows, LANES), F32),
            pltpu.VMEM((rows, width), F32),
            pltpu.VMEM((rows, 2 * LANES), jnp.int32),
            pltpu.VMEM((rows, 2 * LANES), jnp.int32),
            pltpu.VMEM((2, rows, LANES), F32),
            pltpu.VMEM((2, 2, rows, LANES), F32),
            pltpu.VMEM((2, 2, rows, LANES), F32),
            pltpu.VMEM((kept, 2, rows, 2 * LANES), F32),
            pltpu.VMEM((kept, 2, 2, rows, LANES), BF16),
            pltpu.VMEM((kept, 2, 2, rows, LANES), F32),
            pltpu.SemaphoreType.DMA((5, n)),
            pltpu.SemaphoreType.DMA((5, n)),
            pltpu.SemaphoreType.DMA((3, m)),
            pltpu.SemaphoreType.DMA((3, m)),
        ],
        compiler_params=pltpu.CompilerParams(
            collective_id=0, has_side_effects=True, vmem_limit_bytes=40 * 1024 * 1024
        ),
    )(lengths, block_order, tokens, in_gain.reshape(1, width), w_cols, w_out, grad_out)
    uvqk_grad = (
        uv.reshape(chunk, 2, 2, heads_here, head_dim)
        .transpose(0, 3, 2, 1, 4)
        .reshape(chunk, heads_here, 4 * head_dim)
    )
    return tok, uvqk_grad, wo[:, : heads_here * head_dim].T


def solution(mesh):
    in_specs = (
        P("ctx", None),
        P(),
        P(None, "head", None),
        P("head", None),
        P("ctx", None),
        P(),
        P(),
    )
    out_specs = (P("ctx", None), P("ctx", "head", None), P("head", "ctx"))
    return jax.shard_map(body, mesh=mesh, in_specs=in_specs, out_specs=out_specs, check_vma=False)
```

```python
import functools

import jax
import jax.numpy as jnp
from jax import lax
from jax.experimental import pallas as pl
from jax.experimental.pallas import tpu as pltpu
from jax.sharding import PartitionSpec as P

F32 = jnp.float32
BF16 = jnp.bfloat16
LANES = 128
MESH = pl.DeviceIdType.MESH


def dot_nt(a, b):
    return lax.dot_general(a, b, (((1,), (1,)), ((), ())), preferred_element_type=F32)


def dot_nn(a, b):
    return lax.dot_general(a, b, (((1,), (0,)), ((), ())), preferred_element_type=F32)


def dot_tn(a, b):
    return lax.dot_general(a, b, (((0,), (0,)), ((), ())), preferred_element_type=F32)


def silu_parts(scores, scale):
    sigma = 0.5 * jnp.tanh(0.5 * scores) + 0.5
    silu = scores * sigma
    return (silu * scale).astype(BF16), (sigma + silu * (1.0 - sigma)) * scale


def kernel(
    n, m, block, users, score_scale, keep,
    lengths_ref, order_ref, tokens_ref, gain_ref, w_ref, wout_ref, gout_ref,
    tok_ref, uvqk_ref, wo_ref,
    kv_all, q_all, ag_all, st_all, wo_send, wo_recv, uv_send, uv_recv,
    ip_send, ip_recv, tg_all, normed_ref, istd_ref, pre_ref, evq_ref, stq_ref,
    acc_ref, acck_ref, accv_ref, dq_ref, wk_ref, dk_ref,
    c_send, c_recv, h_send, h_recv,
):
    me = lax.axis_index("ctx")
    hd = lax.axis_index("head")
    rows, width = tokens_ref.shape
    half = rows // 2
    part = rows // m
    chunk = width // n

    barrier = pltpu.get_barrier_semaphore()

    def greet_ctx(s, c):
        pl.semaphore_signal(
            barrier, inc=1, device_id={"ctx": lax.rem(me + s, n)}, device_id_type=MESH
        )
        return c

    def greet_head(s, c):
        pl.semaphore_signal(
            barrier, inc=1, device_id={"head": lax.rem(hd + s, m)}, device_id_type=MESH
        )
        return c

    lax.fori_loop(1, n, greet_ctx, 0, unroll=keep)
    lax.fori_loop(1, m, greet_head, 0, unroll=keep)

    def ctx_copy(kind, src, dst, slot, sem, peer):
        return pltpu.make_async_remote_copy(
            src_ref=src.at[slot],
            dst_ref=dst.at[sem],
            send_sem=c_send.at[kind, slot if src is not dst else peer],
            recv_sem=c_recv.at[kind, sem],
            device_id={"ctx": peer},
            device_id_type=MESH,
        )

    def head_copy(kind, src, dst, slot, sem, peer):
        return pltpu.make_async_remote_copy(
            src_ref=src.at[slot],
            dst_ref=dst.at[sem],
            send_sem=h_send.at[kind, slot if src is not dst else peer],
            recv_sem=h_recv.at[kind, sem],
            device_id={"head": peer},
            device_id_type=MESH,
        )

    def spread(copy, kind, src, dst, mine, count, scatter):
        def step(s, c):
            peer = lax.rem(mine + s, count)
            copy(kind, src, dst, peer if scatter else mine, mine, peer).start()
            return c

        lax.fori_loop(1, count, step, 0, unroll=keep)

    def arrived(copy, kind, src, dst, mine, count, scatter, s):
        origin = lax.rem(mine + count - s, count)
        copy(kind, src, dst, origin if scatter else mine, origin, origin).wait_recv()
        return origin

    lines = n // 2
    pair = me + 1 - 2 * lax.rem(me, 2)

    def line_origin(s):
        return lax.rem(me + n - 2 * s, n)

    def pair_origin(s):
        return lax.rem(pair + n - 2 * s, n)

    def hop(kind, buf, slot, sem, peer):
        return pltpu.make_async_remote_copy(
            src_ref=buf.at[slot],
            dst_ref=buf.at[slot],
            send_sem=c_send.at[kind, sem],
            recv_sem=c_recv.at[kind, slot],
            device_id={"ctx": peer},
            device_id_type=MESH,
        )

    def gather(kind, buf):
        def step(s, c):
            peer = lax.rem(me + 2 * s, n)
            hop(kind, buf, me, peer, peer).start()
            return c

        hop(kind, buf, me, pair, pair).start()
        lax.fori_loop(1, lines, step, 0, unroll=keep)

    def relay(kind, buf, s):
        origin = line_origin(s)
        hop(kind, buf, origin, pair_origin(s), pair).wait_recv()
        hop(kind, buf, origin, origin + 1 - 2 * lax.rem(origin, 2), pair).start()

    def relayed(kind, buf, s):
        origin = pair_origin(s)
        hop(kind, buf, origin, origin, pair).wait_recv()

    def sent(copy, kind, src, dst, mine, count, scatter):
        def step(s, c):
            peer = lax.rem(mine + s, count)
            copy(kind, src, dst, peer if scatter else mine, mine, peer).wait_send()
            return c

        lax.fori_loop(1, count, step, 0, unroll=keep)

    x = tokens_ref[...].astype(F32)
    centered = x - jnp.mean(x, axis=1, keepdims=True)
    istd = lax.rsqrt(jnp.mean(centered * centered, axis=1, keepdims=True) + 1e-05)
    normed = centered * istd
    normed_ref[...] = normed
    istd_ref[...] = jnp.broadcast_to(istd, (rows, LANES))
    scaled_in = (normed * gain_ref[...]).astype(BF16)

    def project(cols):
        pre = dot_nn(scaled_in, w_ref[:, cols])
        pre_ref[:, cols] = pre
        return pre * (0.5 * jnp.tanh(0.5 * pre) + 0.5)

    wide_b = project(slice(LANES, 2 * LANES))
    act_b = wide_b.astype(BF16)
    kv_all[me] = act_b
    pl.semaphore_wait(barrier, n + m - 2)
    gather(0, kv_all)
    wide_a = project(slice(0, LANES))
    act_a = wide_a.astype(BF16)
    lane = lax.broadcasted_iota(jnp.int32, (rows, LANES), 1)
    low = lane < 64
    head0 = (lane & 32) == 0
    low_half = lax.broadcasted_iota(jnp.int32, (half, LANES), 1) < 64
    q_all[me] = jnp.where(
        low_half, pltpu.roll(wide_a[:half], 64, 1), wide_a[half:]
    ).astype(BF16)

    gather(1, q_all)

    ends = []
    running = jnp.int32(0)
    for u in range(users):
        running = running + lengths_ref[u]
        ends.append(running)

    def starts(events):
        begin = jnp.zeros_like(events)
        for end in ends:
            begin = jnp.where(events >= end, end, begin)
        return begin

    row = lax.broadcasted_iota(jnp.int32, (rows, 2 * LANES), 0)
    ev_q = jnp.where(
        row < block, order_ref[2 * me] * block + row, (order_ref[2 * me + 1] - 1) * block + row
    )
    evq_ref[...] = ev_q
    stq_ref[...] = starts(ev_q)

    zero_a = jnp.zeros_like(act_a)
    picks_low = [low & head0, low & ~head0]
    picks_high = [(~low) & head0, (~low) & ~head0]
    rolled_b = pltpu.roll(wide_b, 64, 1).astype(BF16)

    def masked(values, picks):
        return [jnp.where(pick, values, zero_a) for pick in picks]

    q_heads = masked(act_a, picks_high)
    units = jnp.where(low, act_a, zero_a).astype(F32)
    gout = gout_ref[...]
    wout_wide = jnp.concatenate([wout_ref[...], jnp.zeros_like(wout_ref[...])], axis=0)
    gated_grad = dot_nt(gout, wout_wide)
    norm_grad = gated_grad * units

    acc_ref[...] = jnp.zeros_like(acc_ref)
    key_lane = lax.broadcasted_iota(jnp.int32, (1, 2 * LANES), 1)

    def query_live(p):
        ev_j = jnp.where(
            key_lane < block,
            order_ref[2 * p] * block + key_lane,
            (order_ref[2 * p + 1] - 1) * block + key_lane,
        )
        live = (ev_j <= evq_ref[...]) & (ev_j >= stq_ref[...])
        return jnp.where(live, score_scale, 0.0)

    def forward(p):
        kv = kv_all[p]
        scale = query_live(p)
        for h in range(2):
            weights, slope = silu_parts(dot_nt(q_heads[h], kv), scale)
            if keep:
                dq_ref[p, h] = slope
            acc_ref[h] += dot_nn(weights, kv)

    lane_half = lax.broadcasted_iota(jnp.int32, (1, LANES), 1)
    k_heads = [masked(rolled_b, picks_low), masked(act_b, picks_high)]
    v_heads = [masked(act_b, picks_low), masked(rolled_b, picks_high)]

    def key_parts(p, part_no):
        ev_i = order_ref[2 * p + part_no] * block + lane_half
        live = (evq_ref[:, :LANES] <= ev_i) & (evq_ref[:, :LANES] >= starts(ev_i))
        scale = jnp.where(live, score_scale, 0.0)
        q = q_all[p]
        return [silu_parts(dot_nt(k_heads[part_no][h], q), scale) for h in range(2)]

    def key_prepare(p):
        if keep:
            for part_no in range(2):
                for h, (weights, slope) in enumerate(key_parts(p, part_no)):
                    wk_ref[p, part_no, h] = weights
                    dk_ref[p, part_no, h] = slope

    def line_step(s, c):
        relay(0, kv_all, s)
        forward(line_origin(s))
        return c

    def pair_step(s, c):
        @pl.when(s > 0)
        def _():
            relay(1, q_all, s)

        key_prepare(line_origin(s))
        relayed(0, kv_all, s)
        forward(pair_origin(s))
        return c

    forward(me)
    lax.fori_loop(1, lines, line_step, 0, unroll=keep)
    lax.fori_loop(0, lines, pair_step, 0, unroll=keep)
    attended = jnp.where(low, jnp.where(head0, acc_ref[0], acc_ref[1]), 0.0)

    def total(v):
        return jnp.sum(v, axis=1, keepdims=True)

    cols = jnp.where(lane == 0, total(attended), 0.0)
    cols = jnp.where(lane == 1, total(attended * attended), cols)
    cols = jnp.where(lane == 2, total(norm_grad), cols)
    cols = jnp.where(lane == 3, total(norm_grad * attended), cols)
    st_all[hd] = jnp.transpose(cols)[:8]
    spread(head_copy, 0, st_all, st_all, hd, m, False)

    def prepare_pair(s, c):
        relayed(1, q_all, s)
        key_prepare(pair_origin(s))
        return c

    early = lines // 2
    lax.fori_loop(0, early, prepare_pair, 0, unroll=keep)

    def stats_in(s, c):
        arrived(head_copy, 0, st_all, st_all, hd, m, False, s)
        return c

    lax.fori_loop(1, m, stats_in, 0, unroll=keep)
    stats = st_all[0]
    for i in range(1, m):
        stats = stats + st_all[i]
    stats = jnp.transpose(jnp.concatenate([stats] * 16, axis=0)) / width
    attn_mean = stats[:, 0:1]
    attn_inv = lax.rsqrt(stats[:, 1:2] - attn_mean * attn_mean + 1e-05)
    grad_mean = stats[:, 2:3]
    cross_mean = (stats[:, 3:4] - attn_mean * grad_mean) * attn_inv
    attn_norm = jnp.where(low, (attended - attn_mean) * attn_inv, 0.0)
    attn_grad = jnp.where(low, (norm_grad - grad_mean - attn_norm * cross_mean) * attn_inv, 0.0)
    ag_all[me] = jnp.where(
        low_half, attn_grad[:half], pltpu.roll(attn_grad[half:], 64, 1)
    ).astype(BF16)
    gather(2, ag_all)

    units_grad = gated_grad * attn_norm
    gated = (attn_norm * units).astype(BF16)
    wo_part = dot_tn(gout, gated).astype(BF16)
    if wo_send.shape[1] != chunk:
        wo_send[...] = jnp.zeros_like(wo_send)
        uv_send[...] = jnp.zeros_like(uv_send)
    for i in range(n):
        wo_send[i, :chunk] = wo_part[i * chunk : (i + 1) * chunk]

    attn_grad = attn_grad.astype(BF16)
    ag_heads = masked(attn_grad, picks_low)
    lax.fori_loop(early, lines, prepare_pair, 0, unroll=keep)

    def relay_grads(s, c):
        relay(2, ag_all, s)
        return c

    lax.fori_loop(1, lines, relay_grads, 0, unroll=keep)
    acc_ref[...] = jnp.zeros_like(acc_ref)

    def query_back(i, c):
        kv = kv_all[pl.ds(2 * i, 2)].reshape(2 * rows, LANES)
        for h in range(2):
            raw = dot_nt(ag_heads[h], kv)
            grads = []
            for b in range(2):
                if keep:
                    slope = dq_ref[2 * i + b, h]
                else:
                    block_kv = kv[b * rows : (b + 1) * rows]
                    _, slope = silu_parts(dot_nt(q_heads[h], block_kv), query_live(2 * i + b))
                grads.append((raw[:, b * rows : (b + 1) * rows] * slope).astype(BF16))
            acc_ref[h] += dot_nn(jnp.concatenate(grads, axis=1), kv)
        return c

    lax.fori_loop(0, lines, query_back, 0, unroll=keep)
    spread(ctx_copy, 3, wo_send, wo_recv, me, n, True)
    query_grad = jnp.where(head0, acc_ref[0], acc_ref[1])

    acck_ref[...] = jnp.zeros_like(acck_ref)
    accv_ref[...] = jnp.zeros_like(accv_ref)

    def key_back(p):
        q = q_all[p]
        ag = ag_all[p]
        for part_no in range(2):
            parts = None if keep else key_parts(p, part_no)
            for h in range(2):
                if keep:
                    weights, slope = wk_ref[p, part_no, h], dk_ref[p, part_no, h]
                else:
                    weights, slope = parts[h]
                score_grad = (dot_nt(v_heads[part_no][h], ag) * slope).astype(BF16)
                acck_ref[part_no, h] += dot_nn(score_grad, q)
                accv_ref[part_no, h] += dot_nn(weights, ag)

    def line_back(s, c):
        key_back(line_origin(s))
        return c

    def pair_back(s, c):
        relayed(2, ag_all, s)
        key_back(pair_origin(s))
        return c

    lax.fori_loop(0, lines, line_back, 0, unroll=keep)
    lax.fori_loop(0, lines, pair_back, 0, unroll=keep)

    def fold(acc, part_no):
        return jnp.where(head0, acc[part_no, 0], acc[part_no, 1])

    key_grad = pltpu.roll(fold(acck_ref, 0), 64, 1) + fold(acck_ref, 1)
    value_grad = fold(accv_ref, 0) + pltpu.roll(fold(accv_ref, 1), 64, 1)
    act_grad = jnp.concatenate(
        [jnp.where(low, units_grad, query_grad), jnp.where(low, value_grad, key_grad)], axis=1
    )
    pre = pre_ref[...]
    sig = 0.5 * jnp.tanh(0.5 * pre) + 0.5
    pre_grad = (act_grad * (sig * (1.0 + pre * (1.0 - sig)))).astype(BF16)
    input_part = dot_nt(pre_grad, w_ref[...]).astype(BF16)
    for i in range(m):
        ip_send[i] = input_part[i * part : (i + 1) * part]
    spread(head_copy, 1, ip_send, ip_recv, hd, m, True)

    scaled_in = (normed_ref[...] * gain_ref[...]).astype(BF16)
    uv_part = dot_tn(scaled_in, pre_grad).astype(BF16)
    for i in range(n):
        uv_send[i, :chunk] = uv_part[i * chunk : (i + 1) * chunk]
    spread(ctx_copy, 4, uv_send, uv_recv, me, n, True)

    def parts_in(s, summed):
        origin = arrived(head_copy, 1, ip_send, ip_recv, hd, m, True, s)
        return summed + ip_recv[origin].astype(F32)

    input_grad = lax.fori_loop(1, m, parts_in, ip_send[hd].astype(F32), unroll=keep)
    mine = pl.ds(pl.multiple_of(hd * part, part), part)
    scaled_grad = input_grad * gain_ref[...]
    my_normed = normed_ref[mine]
    my_istd = istd_ref[mine][:, 0:1]
    mean_a = jnp.mean(scaled_grad, axis=1, keepdims=True)
    mean_b = jnp.mean(scaled_grad * my_normed, axis=1, keepdims=True)
    tg_all[hd] = (
        gout_ref[mine].astype(F32) + (scaled_grad - mean_a - my_normed * mean_b) * my_istd
    ).astype(BF16)
    spread(head_copy, 2, tg_all, tg_all, hd, m, False)

    def wo_in(s, summed):
        origin = arrived(ctx_copy, 3, wo_send, wo_recv, me, n, True, s)
        return summed + wo_recv[origin].astype(F32)

    wo_sum = lax.fori_loop(1, n, wo_in, wo_send[me].astype(F32), unroll=keep)
    wo_ref[...] = wo_sum[:chunk]

    def uv_in(s, summed):
        origin = arrived(ctx_copy, 4, uv_send, uv_recv, me, n, True, s)
        return summed + uv_recv[origin].astype(F32)

    uv_sum = lax.fori_loop(1, n, uv_in, uv_send[me].astype(F32), unroll=keep)
    uvqk_ref[...] = uv_sum[:chunk]

    def tokens_in(s, c):
        arrived(head_copy, 2, tg_all, tg_all, hd, m, False, s)
        return c

    lax.fori_loop(1, m, tokens_in, 0, unroll=keep)
    for i in range(m):
        tok_ref[i * part : (i + 1) * part] = tg_all[i]

    sent(ctx_copy, 0, kv_all, kv_all, me, n, False)
    sent(ctx_copy, 1, q_all, q_all, me, n, False)
    sent(ctx_copy, 2, ag_all, ag_all, me, n, False)
    sent(ctx_copy, 3, wo_send, wo_recv, me, n, True)
    sent(ctx_copy, 4, uv_send, uv_recv, me, n, True)
    sent(head_copy, 0, st_all, st_all, hd, m, False)
    sent(head_copy, 1, ip_send, ip_recv, hd, m, True)
    sent(head_copy, 2, tg_all, tg_all, hd, m, False)


def body(tokens, in_gain, w_uvqk, w_out, grad_out, lengths, block_order):
    rows, width = tokens.shape
    n = lax.axis_size("ctx")
    m = lax.axis_size("head")
    heads_here = w_uvqk.shape[1]
    head_dim = w_uvqk.shape[2] // 4
    total = rows * n
    block = total // block_order.shape[0]
    chunk = width // n
    padded = max(chunk, 16)
    keep = n <= 16
    kept = n if keep else 1
    w_cols = (
        w_uvqk.reshape(width, heads_here, 2, 2, head_dim)
        .transpose(0, 3, 2, 1, 4)
        .reshape(width, width)
    )
    vmem = pl.BlockSpec(memory_space=pltpu.VMEM)
    smem = pl.BlockSpec(memory_space=pltpu.SMEM)
    tok, uv, wo = pl.pallas_call(
        functools.partial(
            kernel, n, m, block, lengths.shape[0], 1.0 / (total // 2), keep
        ),
        out_shape=(
            jax.ShapeDtypeStruct((rows, width), BF16),
            jax.ShapeDtypeStruct((chunk, width), F32),
            jax.ShapeDtypeStruct((chunk, LANES), F32),
        ),
        in_specs=[smem, smem] + [vmem] * 5,
        out_specs=(vmem, vmem, vmem),
        scratch_shapes=[
            pltpu.VMEM((n, rows, LANES), BF16),
            pltpu.VMEM((n, rows // 2, LANES), BF16),
            pltpu.VMEM((n, rows // 2, LANES), BF16),
            pltpu.VMEM((m, 8, rows), F32),
            pltpu.VMEM((n, padded, LANES), BF16),
            pltpu.VMEM((n, padded, LANES), BF16),
            pltpu.VMEM((n, padded, width), BF16),
            pltpu.VMEM((n, padded, width), BF16),
            pltpu.VMEM((m, rows // m, width), BF16),
            pltpu.VMEM((m, rows // m, width), BF16),
            pltpu.VMEM((m, rows // m, width), BF16),
            pltpu.VMEM((rows, width), F32),
            pltpu.VMEM((rows, LANES), F32),
            pltpu.VMEM((rows, width), F32),
            pltpu.VMEM((rows, 2 * LANES), jnp.int32),
            pltpu.VMEM((rows, 2 * LANES), jnp.int32),
            pltpu.VMEM((2, rows, LANES), F32),
            pltpu.VMEM((2, 2, rows, LANES), F32),
            pltpu.VMEM((2, 2, rows, LANES), F32),
            pltpu.VMEM((kept, 2, rows, 2 * LANES), F32),
            pltpu.VMEM((kept, 2, 2, rows, LANES), BF16),
            pltpu.VMEM((kept, 2, 2, rows, LANES), F32),
            pltpu.SemaphoreType.DMA((5, n)),
            pltpu.SemaphoreType.DMA((5, n)),
            pltpu.SemaphoreType.DMA((3, m)),
            pltpu.SemaphoreType.DMA((3, m)),
        ],
        compiler_params=pltpu.CompilerParams(
            collective_id=0, has_side_effects=True, vmem_limit_bytes=40 * 1024 * 1024
        ),
    )(lengths, block_order, tokens, in_gain.reshape(1, width), w_cols, w_out, grad_out)
    uvqk_grad = (
        uv.reshape(chunk, 2, 2, heads_here, head_dim)
        .transpose(0, 3, 2, 1, 4)
        .reshape(chunk, heads_here, 4 * head_dim)
    )
    return tok, uvqk_grad, wo[:, : heads_here * head_dim].T


def solution(mesh):
    in_specs = (
        P("ctx", None),
        P(),
        P(None, "head", None),
        P("head", None),
        P("ctx", None),
        P(),
        P(),
    )
    out_specs = (P("ctx", None), P("ctx", "head", None), P("head", "ctx"))
    return jax.shard_map(body, mesh=mesh, in_specs=in_specs, out_specs=out_specs, check_vma=False)
```
